32 devices in a mesh: row: 2 (over y), col: 4 (over z), leaf: 4 (over x, core).
Axes of the slice: x: 2, y: 2, z: 4, core: 2. Of those that a mesh axis runs over, the one named last changes fastest.
Arguments:
- rhs_leaf: float32 [4, 8192, 128], P('leaf', 'row'), may hold values from -6 to 6
- rhs_mid: float32 [2, 8192, 128], P(None, 'row'), may hold values from -6 to 6
- rhs_root: float32 [8192, 128], P('row'), may hold values from -6 to 6
- inverse_leaf: bfloat16 [4, 8192, 8192], P('leaf', 'col', 'row'), may hold values from -3 to 3, as said below
- inverse_mid: bfloat16 [2, 8192, 8192], P(None, ('col', 'leaf'), 'row'), may hold values from -3 to 3, as said below
- inverse_root: bfloat16 [8192, 8192], P(('col', 'leaf'), 'row'), may hold values from -3 to 3, as said below
- factor_leaf_mid: bfloat16 [4, 8192, 8192], P('leaf', 'row', 'col'), may hold values from -0.0625 to 0.0625
- factor_leaf_root: bfloat16 [4, 8192, 8192], P('leaf', 'row', 'col'), may hold values from -0.0625 to 0.0625
- factor_mid_root: bfloat16 [2, 8192, 8192], P(None, 'row', ('col', 'leaf')), may hold values from -0.0625 to 0.0625
- pattern_leaf_mid: int32 [4, 32, 32], P('leaf', 'row', 'col'), may hold values 0 or 1
- pattern_leaf_root: int32 [4, 32, 32], P('leaf', 'row', 'col'), may hold values 0 or 1
- pattern_mid_root: int32 [2, 32, 32], P(None, 'row', ('col', 'leaf')), may hold values 0 or 1
Outputs:
- solve_leaf: float32 [4, 8192, 128], P('leaf', 'row')
- solve_mid: float32 [2, 8192, 128], P(None, 'row')
- solve_root: float32 [8192, 128], P('row')
- forward_root: float32 [8192, 128], P(('col', 'leaf'))
The draws below stay inside these ranges and needn't reach their ends.
Inputs may be any that keep to these rules, and one draw needn't show every extreme that they name: `inverse_leaf`: lower triangular, with a positive diagonal. `inverse_mid`: lower triangular, with a positive diagonal. `inverse_root`: lower triangular, with a positive diagonal.
All inputs are finite; a program needn't handle non-finite values. No bound on the sum of `pattern_leaf_mid` or of `pattern_leaf_root` or of `pattern_mid_root` on one device may be relied on, other than what follows from the above.
Results may differ from the reference program's by a relative error of at most 0.018.
Values sent between devices are 32-bit elements; how exact they have to be, the bound alone decides.
No kernel may reach another device: no remote copies, remote signals or barrier semaphores. Data moves between devices by JAX's collectives and lax.ppermute only.
A program may use at most 256 MiB of HBM per device.

```python
import math
import jax
import jax.numpy as jnp
from jax import lax

SB = 32
NRHS = 128
S = 8192


def lower_draw(key, leading, extent):
    key_values, key_diagonal = jax.random.split(key, 2)
    array_shape = leading + (extent, extent)
    values = jax.random.normal(key_values, array_shape, jnp.float32)
    diagonal = jax.random.uniform(key_diagonal, leading + (extent,), jnp.float32, 0.6, 1.4)
    row_index = lax.broadcasted_iota(jnp.int32, (extent, extent), 0)
    col_index = lax.broadcasted_iota(jnp.int32, (extent, extent), 1)
    strict = jnp.where(row_index > col_index, values * (0.8 / math.sqrt(extent)), 0.0)
    matrix_out = strict + jnp.where(row_index == col_index, 1.0, 0.0) * diagonal[..., :, None]
    return matrix_out


def draw_inverse_leaf(key, part):
    return lower_draw(jax.random.fold_in(key, 11), (4,), S).astype(jnp.bfloat16)


def draw_inverse_mid(key, part):
    return lower_draw(jax.random.fold_in(key, 12), (2,), S).astype(jnp.bfloat16)


def draw_inverse_root(key, part):
    return lower_draw(jax.random.fold_in(key, 13), (), S).astype(jnp.bfloat16)


def with_ends(drawn, stream_key, low, top_value):
    longest = drawn.shape.index(max(drawn.shape))
    spots = []
    for shift in (0, 1):
        where = [jax.random.randint(jax.random.fold_in(stream_key, axis), (), 0, length) for axis, length in enumerate(drawn.shape)]
        where[longest] = (where[longest] + shift) % drawn.shape[longest]
        spots.append(tuple(where))
    return drawn.at[spots[0]].set(low).at[spots[1]].set(top_value)


def steps_of(rng, shape, cuts, smallest, high):
    loudness = 1.0
    for position, blocks in cuts:
        heights = jax.random.uniform(jax.random.fold_in(jax.random.fold_in(rng, 6), position), (blocks,), jnp.float32, smallest / len(cuts), high / len(cuts))
        loudness = loudness * jnp.repeat(jnp.exp(heights), shape[position] // blocks).reshape((-1,) + (1,) * (len(shape) - 1 - position))
    return loudness


def noise(own_key, shape, spread, reach, pieces=(), kind=jnp.bfloat16):
    factor_of = steps_of(own_key, shape, pieces, -0.22, 0.18) if pieces else 1.0
    drawn = jax.random.normal(own_key, shape, jnp.float32) * spread * factor_of
    return jnp.minimum(jnp.maximum(drawn, -reach), reach).astype(kind)


def setup_inputs(seed: int = 0) -> dict:
    streams_of = jax.random.split(jax.random.key(seed), 13)
    rhs_leaf = noise(streams_of[0], (4, S, NRHS), 1.0, 6.0, ((0, 4), (1, 2)), jnp.float32)
    rhs_mid = noise(streams_of[1], (2, S, NRHS), 1.0, 6.0, ((1, 2),), jnp.float32)
    rhs_root = noise(streams_of[2], (S, NRHS), 1.0, 6.0, ((0, 2),), jnp.float32)
    inverse_leaf = draw_inverse_leaf(jax.random.fold_in(streams_of[12], 71), 0)
    inverse_mid = draw_inverse_mid(jax.random.fold_in(streams_of[12], 71), 0)
    inverse_root = draw_inverse_root(jax.random.fold_in(streams_of[12], 71), 0)
    factor_leaf_mid = noise(streams_of[6], (4, S, S), S ** -0.5, 0.0625, ((0, 4), (1, 2), (2, 4)))
    factor_leaf_root = noise(streams_of[7], (4, S, S), S ** -0.5, 0.0625, ((0, 4), (1, 2), (2, 4)))
    factor_mid_root = noise(streams_of[8], (2, S, S), S ** -0.5, 0.0625, ((1, 2), (2, 16)))
    pattern_leaf_mid = with_ends((jax.random.randint(streams_of[9], (4, SB, SB), 0, 4) < 3).astype(jnp.int32), jax.random.fold_in(streams_of[9], 1), 0, 1)
    pattern_leaf_root = with_ends((jax.random.randint(streams_of[10], (4, SB, SB), 0, 4) < 3).astype(jnp.int32), jax.random.fold_in(streams_of[10], 1), 0, 1)
    pattern_mid_root = with_ends((jax.random.randint(streams_of[11], (2, SB, SB), 0, 4) < 3).astype(jnp.int32), jax.random.fold_in(streams_of[11], 1), 0, 1)
    return dict(rhs_leaf=rhs_leaf, rhs_mid=rhs_mid, rhs_root=rhs_root, inverse_leaf=inverse_leaf, inverse_mid=inverse_mid, inverse_root=inverse_root, factor_leaf_mid=factor_leaf_mid, factor_leaf_root=factor_leaf_root, factor_mid_root=factor_mid_root, pattern_leaf_mid=pattern_leaf_mid, pattern_leaf_root=pattern_leaf_root, pattern_mid_root=pattern_mid_root)


def masked_blocks(matrix, pattern):
    leading = matrix.shape[:-2]
    row_count, col_count = matrix.shape[-2], matrix.shape[-1]
    block_rows, block_cols = pattern.shape[-2], pattern.shape[-1]
    tiles = matrix.reshape(leading + (block_rows, row_count // block_rows, block_cols, col_count // block_cols))
    keeper = pattern.astype(matrix.dtype)[..., :, None, :, None]
    return (tiles * keeper).reshape(matrix.shape)


def product(matrix, vector):
    return jnp.einsum("pij,pjk->pik", matrix.astype(jnp.float32), vector.astype(jnp.float32))


def transposed(matrix, vector):
    return jnp.einsum("pji,pjk->pik", matrix.astype(jnp.float32), vector.astype(jnp.float32))


def reference(rhs_leaf, rhs_mid, rhs_root, inverse_leaf, inverse_mid, inverse_root, factor_leaf_mid, factor_leaf_root, factor_mid_root, pattern_leaf_mid, pattern_leaf_root, pattern_mid_root):
    leaf_mid = masked_blocks(factor_leaf_mid, pattern_leaf_mid)
    leaf_root = masked_blocks(factor_leaf_root, pattern_leaf_root)
    mid_root = masked_blocks(factor_mid_root, pattern_mid_root)
    forward_leaf = product(inverse_leaf, rhs_leaf.astype(jnp.bfloat16))
    leaf_half = forward_leaf.astype(jnp.bfloat16)
    to_mid = product(leaf_mid, leaf_half)
    mid_terms = to_mid.reshape((2, 2) + to_mid.shape[1:]).sum(axis=1)
    residue_mid = rhs_mid - mid_terms
    forward_mid = product(inverse_mid, residue_mid.astype(jnp.bfloat16))
    mid_half = forward_mid.astype(jnp.bfloat16)
    root_terms = jnp.sum(product(leaf_root, leaf_half), axis=0) + jnp.sum(product(mid_root, mid_half), axis=0)
    residue_root = rhs_root - root_terms
    forward_root = product(inverse_root[None], residue_root.astype(jnp.bfloat16)[None])
    solve_root = transposed(inverse_root[None], forward_root.astype(jnp.bfloat16))[0]
    root_back = solve_root.astype(jnp.bfloat16)
    corrected_mid = forward_mid - jnp.einsum("pji,jk->pik", mid_root.astype(jnp.float32), root_back.astype(jnp.float32))
    solve_mid = transposed(inverse_mid, corrected_mid.astype(jnp.bfloat16))
    mid_back = jnp.repeat(solve_mid.astype(jnp.bfloat16), 2, axis=0)
    corrected_leaf = forward_leaf - transposed(leaf_mid, mid_back) - jnp.einsum("pji,jk->pik", leaf_root.astype(jnp.float32), root_back.astype(jnp.float32))
    solve_leaf = transposed(inverse_leaf, corrected_leaf.astype(jnp.bfloat16))
    return solve_leaf, solve_mid, solve_root, forward_root[0]
```

```python
import jax
import jax.numpy as jnp
from jax import lax
from jax.sharding import PartitionSpec as P


def masked_blocks(matrix, pattern):
    leading, row_count, col_count = matrix.shape
    block_rows = pattern.shape[1]
    block_cols = pattern.shape[2]
    tiles = matrix.reshape(
        leading, block_rows, row_count // block_rows, block_cols, col_count // block_cols
    )
    keeper = pattern.astype(matrix.dtype)[:, :, None, :, None]
    return (tiles * keeper).reshape(leading, row_count, col_count)


def send_xor(value, axis, size, bit):
    return lax.ppermute(value, axis, [(i, i ^ bit) for i in range(size)])


def pick(blocks, index):
    return lax.dynamic_index_in_dim(blocks, index, 0, keepdims=False)


def scatter_sum(value, axis, size, bits):
    me = lax.axis_index(axis)
    count = len(bits) + 1
    unit = bits[0]
    slot = (me // unit) % count
    blocks = value.reshape((count, value.shape[0] // count) + value.shape[1:])
    total = pick(blocks, slot)
    arrived = [
        send_xor(pick(blocks, slot ^ (bit // unit)), axis, size, bit) for bit in bits
    ]
    for block in arrived:
        total = total + block
    return total


def gather_all(value, axis, size, bits):
    me = lax.axis_index(axis)
    count = len(bits) + 1
    unit = bits[0]
    slot = (me // unit) % count
    out = jnp.zeros((count,) + value.shape, value.dtype)
    out = lax.dynamic_update_index_in_dim(out, value, slot, 0)
    for bit in bits:
        block = send_xor(value, axis, size, bit)
        out = lax.dynamic_update_index_in_dim(out, block, slot ^ (bit // unit), 0)
    return out.reshape((count * value.shape[0],) + value.shape[1:])


def make_shards(sizes):
    rows, cols, leaves = sizes["row"], sizes["col"], sizes["leaf"]
    col_bits = list(range(1, cols))

    def row_total(partial_sum):
        if rows == 2:
            return partial_sum + send_xor(partial_sum, "row", rows, 1)
        return lax.psum(partial_sum, "row")

    def col_scatter(value):
        return scatter_sum(value, "col", cols, col_bits)

    def col_gather(value):
        return gather_all(value, "col", cols, col_bits)

    def leaf_scatter(value, bit):
        return scatter_sum(value, "leaf", leaves, [bit])

    def leaf_gather(value, bit):
        return gather_all(value, "leaf", leaves, [bit])

    def dot(a, b):
        return jnp.dot(a, b, preferred_element_type=jnp.float32)

    def dot_t(a, b):
        return jnp.einsum("ji,jk->ik", a, b, preferred_element_type=jnp.float32)

    def half(a):
        return a.astype(jnp.bfloat16)

    def shards(
        rhs_leaf,
        rhs_mid,
        rhs_root,
        inverse_leaf,
        inverse_mid,
        inverse_root,
        factor_leaf_mid,
        factor_leaf_root,
        factor_mid_root,
        pattern_leaf_mid,
        pattern_leaf_root,
        pattern_mid_root,
    ):
        leaf_mid = masked_blocks(factor_leaf_mid, pattern_leaf_mid)[0]
        leaf_root = masked_blocks(factor_leaf_root, pattern_leaf_root)[0]
        mid_root = masked_blocks(factor_mid_root, pattern_mid_root)
        leaf_inverse = inverse_leaf[0]
        leaf = lax.axis_index("leaf")
        owner = leaf // 2

        forward_leaf = row_total(dot(leaf_inverse, half(rhs_leaf[0])))
        leaf_half = half(forward_leaf)
        to_mid = col_scatter(leaf_scatter(dot(leaf_mid, leaf_half), 1))
        to_root = dot(leaf_root, leaf_half)
        to_mid = leaf_gather(leaf_gather(col_gather(to_mid)[None], 2)[None], 1)
        residue_mid = rhs_mid - jnp.swapaxes(to_mid, 0, 1).reshape(rhs_mid.shape)
        forward_mid = row_total(
            jnp.einsum(
                "pij,pjk->pik", inverse_mid, half(residue_mid), preferred_element_type=jnp.float32
            )
        )
        root_partial = to_root + jnp.einsum(
            "pij,pjk->ik", mid_root, half(forward_mid), preferred_element_type=jnp.float32
        )
        to_root = col_scatter(leaf_scatter(leaf_scatter(root_partial, 1), 2))
        residue_root = rhs_root - leaf_gather(leaf_gather(col_gather(to_root), 2), 1)
        forward_root = row_total(dot(inverse_root, half(residue_root)))

        root_terms = dot_t(inverse_root, half(forward_root))
        root_terms = col_scatter(leaf_scatter(leaf_scatter(root_terms, 1), 2))
        solve_root = leaf_gather(leaf_gather(col_gather(root_terms), 2), 1)
        root_back = half(solve_root)
        corrected_mid = forward_mid - row_total(
            jnp.einsum("pji,jk->pik", mid_root, root_back, preferred_element_type=jnp.float32)
        )
        mid_terms = jnp.einsum(
            "pji,pjk->pik", inverse_mid, half(corrected_mid), preferred_element_type=jnp.float32
        )
        mid_rows = mid_terms.shape[1]
        mid_terms = mid_terms.reshape((2, 2, mid_rows // 2, -1)).swapaxes(0, 1)
        mid_terms = leaf_scatter(mid_terms, 1)[0]
        mid_terms = leaf_scatter(mid_terms, 2)[0]
        mid_own = leaf_gather(col_gather(col_scatter(mid_terms)), 1)
        mid_other = send_xor(mid_own, "leaf", leaves, 2)
        solve_mid = jnp.where(
            owner == 0, jnp.stack([mid_own, mid_other]), jnp.stack([mid_other, mid_own])
        )
        back_partial = dot_t(leaf_mid, half(mid_own)) + dot_t(leaf_root, root_back)
        corrected_leaf = forward_leaf - row_total(back_partial)
        leaf_terms = dot_t(leaf_inverse, half(corrected_leaf))
        solve_leaf = col_gather(col_scatter(leaf_terms))[None]
        return (solve_leaf, solve_mid, solve_root, forward_root)

    return shards


def solution(mesh):
    return jax.shard_map(
        make_shards(dict(mesh.shape)),
        mesh=mesh,
        in_specs=(
            P("leaf", "row", None),
            P(None, "row", None),
            P("row", None),
            P("leaf", "col", "row"),
            P(None, ("col", "leaf"), "row"),
            P(("col", "leaf"), "row"),
            P("leaf", "row", "col"),
            P("leaf", "row", "col"),
            P(None, "row", ("col", "leaf")),
            P("leaf", "row", "col"),
            P("leaf", "row", "col"),
            P(None, "row", ("col", "leaf")),
        ),
        out_specs=(
            P("leaf", "row", None),
            P(None, "row", None),
            P("row", None),
            P(("col", "leaf"), None),
        ),
        check_vma=False,
    )
```

```python
import functools

import jax
import jax.numpy as jnp
from jax import lax
from jax.experimental import pallas as pl
from jax.experimental.pallas import tpu as pltpu
from jax.sharding import PartitionSpec as P

HALF = jnp.bfloat16
FULL = jnp.float32


def product_kernel(cfg, *refs):
    refs = list(refs)
    tile_p, tile_r, dst, offs, pattern = refs[:5]
    matrix = refs[5]
    at = 6
    terms = refs[at : at + len(cfg["signs"])]
    at += len(cfg["signs"])
    pieces = refs[at : at + cfg["pieces"]]
    at += cfg["pieces"]
    addend = refs[at] if cfg["addend"] else None
    at += 1 if cfg["addend"] else 0
    out = refs[at]
    at += 1
    ordered = refs[at] if cfg["ordered"] else None
    at += 1 if cfg["ordered"] else 0
    vector = refs[at]
    transposed, depth, vectors = cfg["transposed"], cfg["depth"], cfg["vectors"]
    step = pl.program_id(0)

    @pl.when(step == 0)
    def _():
        if pieces:
            target = ordered if transposed else vector
            count = 0
            for piece in pieces:
                size = cfg["piece"]
                for n in range(piece.shape[0] // size):
                    row = pl.multiple_of(offs[count], size)
                    target[pl.ds(row, size), :] = piece[pl.ds(n * size, size), :].astype(
                        target.dtype
                    )
                    count += 1
        chunk = min(512, depth)
        for base in range(0, vectors * depth, chunk):
            if pieces:
                if not transposed:
                    break
                value = ordered[pl.ds(base, chunk), :]
            else:
                value = None
                for term, sign in zip(terms, cfg["signs"]):
                    part = term[pl.ds(base, chunk), :].astype(FULL)
                    if value is None:
                        value = part
                    else:
                        value = value + part if sign > 0 else value - part
            if transposed:
                which, column = base // depth, base % depth
                vector[pl.ds(which * 128, 128), pl.ds(column, chunk)] = value.T.astype(HALF)
            else:
                vector[pl.ds(base, chunk), :] = value.astype(HALF)

    tile, granule, block = cfg["tile"], cfg["granule"], cfg["block"]
    blocks_r, blocks_c, other = cfg["blocks_r"], cfg["blocks_c"], cfg["other"]
    for sub in range(tile // block):
        result = None
        for lead in range(matrix.shape[0]):
            index = lead if cfg["sum_p"] else tile_p[step]
            start = 0
            if vectors > 1:
                stride = 128 if transposed else depth
                start = index * stride
                if not cfg["sum_p"]:
                    start = pl.multiple_of(start, stride)
            if transposed:
                x = vector[pl.ds(start, 128), :]
                a = matrix[lead, :, pl.ds(sub * block, block)]
            else:
                x = vector[pl.ds(start, depth), :]
                a = matrix[lead, pl.ds(sub * block, block), :]
            if cfg["masked"]:
                here = (tile_r[step] * tile + sub * block) // cfg["pattern_block"]
                kept = []
                for n in range(depth // other):
                    if transposed:
                        flag = pattern[(index * blocks_r + n) * blocks_c + here]
                        part = x[:, n * other : (n + 1) * other]
                    else:
                        flag = pattern[(index * blocks_r + here) * blocks_c + n]
                        part = x[n * other : (n + 1) * other, :]
                    kept.append((part.astype(FULL) * flag.astype(FULL)).astype(HALF))
                if len(kept) > 1:
                    x = jnp.concatenate(kept, axis=1 if transposed else 0)
                else:
                    x = kept[0]
            if transposed:
                term = jnp.dot(x, a, preferred_element_type=FULL)
            else:
                term = jnp.dot(a, x, preferred_element_type=FULL)
            result = term if result is None else result + term
        if transposed:
            result = result.T
        for g in range(block // granule):
            row = pl.multiple_of(dst[step * (tile // granule) + sub * (block // granule) + g], granule)
            value = result[g * granule : (g + 1) * granule, :]
            if addend is not None:
                value = value + addend[pl.ds(row, granule), :]
            out[pl.ds(row, granule), :] = value


def product(
    matrix,
    *,
    transposed=False,
    terms=(),
    pieces=(),
    piece=0,
    offs=None,
    tile_p=None,
    tile_r=None,
    tile=None,
    dst=None,
    granule=None,
    pattern=None,
    sum_p=False,
    addend=None,
    ordered=False,
    vectors=1,
):
    lead, rows, cols = matrix.shape
    extent, depth = (cols, rows) if transposed else (rows, cols)
    tiles = tile_r.shape[0]
    out_rows = tiles * tile
    masked = pattern is not None
    block, other, pattern_block = tile, depth, tile
    blocks_r = blocks_c = 1
    if masked:
        blocks_r, blocks_c = pattern.shape[1:]
        pattern_block = extent // (blocks_c if transposed else blocks_r)
        other = depth // (blocks_r if transposed else blocks_c)
        block = min(tile, pattern_block)
        flags = pattern.reshape(-1)
    else:
        flags = jnp.zeros((8,), jnp.int32)
        if transposed:
            block = min(tile, 256)
    granule = min(granule or block, block)
    if dst is None:
        dst = jnp.arange(out_rows // granule, dtype=jnp.int32) * granule
    if offs is None:
        offs = jnp.zeros((8,), jnp.int32)
    if tile_p is None:
        tile_p = jnp.zeros((tiles,), jnp.int32)
    signs = tuple(sign for _, sign in terms)
    term_arrays = [array for array, _ in terms]
    x_rows = vectors * depth
    cfg = dict(
        transposed=transposed, depth=depth, vectors=vectors, signs=signs, pieces=len(pieces),
        piece=piece, addend=addend is not None, ordered=ordered, tile=tile, granule=granule,
        block=block, other=other, pattern_block=pattern_block, blocks_r=blocks_r,
        blocks_c=blocks_c, masked=masked, sum_p=sum_p,
    )
    held = lead if sum_p else 1
    if transposed:
        matrix_block = (held, depth, tile)
        matrix_map = lambda t, tp, tr, *_: (tp[t], 0, tr[t])
    else:
        matrix_block = (held, tile, depth)
        matrix_map = lambda t, tp, tr, *_: (tp[t], tr[t], 0)

    def whole(array):
        return pl.BlockSpec(array.shape, lambda t, *_: (0, 0), pipeline_mode=pl.Buffered(1))

    inputs = term_arrays + list(pieces) + ([addend] if addend is not None else [])
    out_shape = [jax.ShapeDtypeStruct((out_rows, 128), FULL)]
    out_specs = [pl.BlockSpec((out_rows, 128), lambda t, *_: (0, 0))]
    if ordered:
        out_shape.append(jax.ShapeDtypeStruct((x_rows, 128), FULL))
        out_specs.append(pl.BlockSpec((x_rows, 128), lambda t, *_: (0, 0)))
    scratch = (vectors * 128, depth) if transposed else (x_rows, 128)
    matrix_bytes = held * depth * tile * 2
    resident = sum(a.size * a.dtype.itemsize for a in inputs)
    written = sum(s.size * 4 for s in out_shape)
    budget = 2 * matrix_bytes + resident + 2 * written + x_rows * 256 + (12 << 20)
    budget = max(budget, 57 << 20)
    result = pl.pallas_call(
        functools.partial(product_kernel, cfg),
        grid_spec=pltpu.PrefetchScalarGridSpec(
            num_scalar_prefetch=5,
            grid=(tiles,),
            in_specs=[pl.BlockSpec(matrix_block, matrix_map)] + [whole(a) for a in inputs],
            out_specs=out_specs,
            scratch_shapes=[pltpu.VMEM(scratch, HALF)],
        ),
        out_shape=out_shape,
        compiler_params=pltpu.CompilerParams(vmem_limit_bytes=int(budget)),
        cost_estimate=pl.CostEstimate(
            flops=2 * tiles * tile * depth * held * 128,
            bytes_accessed=tiles * matrix_bytes + resident + written,
            transcendentals=0,
        ),
    )(tile_p, tile_r, dst, offs, flags, matrix, *inputs)
    return tuple(result) if ordered else result[0]


def ints(values):
    return jnp.stack([jnp.asarray(v, jnp.int32) for v in values]).reshape(-1)


def make_shards(sizes):
    rows, cols, leaves = sizes["row"], sizes["col"], sizes["leaf"]

    def send(value, axis, bit):
        size = sizes[axis]
        return lax.ppermute(value, axis, [(i, i ^ bit) for i in range(size)])

    def row_terms(part, sign=1):
        if rows == 2:
            return [(part, sign), (send(part, "row", 1), sign)]
        return [(lax.psum(part, "row"), sign)]

    def total(terms):
        value = terms[0][0]
        for term, sign in terms[1:]:
            value = value + term if sign > 0 else value - term
        return value

    def col_reduce(blocks):
        value = blocks[0]
        for k, block in [(k, send(blocks[k], "col", k)) for k in range(1, cols)]:
            value = value + block
        return value

    def col_collect(value):
        return [value] + [send(value, "col", k) for k in range(1, cols)]

    def shards(
        rhs_leaf,
        rhs_mid,
        rhs_root,
        inverse_leaf,
        inverse_mid,
        inverse_root,
        factor_leaf_mid,
        factor_leaf_root,
        factor_mid_root,
        pattern_leaf_mid,
        pattern_leaf_root,
        pattern_mid_root,
    ):
        leaf = lax.axis_index("leaf")
        col = lax.axis_index("col")
        owner = leaf // 2
        parity = leaf % 2
        inverse_root = inverse_root[None]
        full = rhs_root.shape[0]
        split = full // 2
        cut_mid = split // cols
        cut_root = cut_mid // 2
        own = inverse_mid.shape[1]
        unit = full // pattern_leaf_mid.shape[1]

        def tiles(count, start=0):
            return jnp.arange(count, dtype=jnp.int32) + start

        def fit(extent, limit):
            return min(extent, limit)

        def half_start(i, tile):
            return (parity ^ i) * (split // tile)

        def order(sub, granule, with_pair):
            pairs = 2 if with_pair else 1
            spots = []
            for j in range(pairs):
                for k in range(cols):
                    spot = (((j ^ owner) if with_pair else 0) * cols + (k ^ col)) * sub
                    spots += [spot + n * granule for n in range(sub // granule)]
            return ints(spots)

        def pair_sum(make):
            there = make(1)
            arrived = send(there, "leaf", 1)
            return make(0), arrived

        def plane_reduce(here, arrived, cut):
            shape = (2, cols, cut, 128)
            here, arrived = here.reshape(shape), arrived.reshape(shape)
            first = min(max(8, (2 * cut // 3 + 4) // 8 * 8), cut - 8)
            rest = cut - first

            def part(j, k, low, high):
                return here[j, k, low:high] + arrived[j, k, low:high]

            across = send(
                (here[1, :, :first] + arrived[1, :, :first]).reshape(cols * first, 128), "leaf", 2
            )
            moved = [
                send(
                    (here[:, k, first:] + arrived[:, k, first:]).reshape(2 * rest, 128), "col", k
                )
                for k in range(1, cols)
            ]
            near = [
                part(0, k, 0, first) + across[k * first : (k + 1) * first] for k in range(cols)
            ]
            low = col_reduce(near)
            far = part(1, 0, first, cut)
            high = part(0, 0, first, cut)
            for block in moved:
                far = far + block[rest:]
                high = high + block[:rest]
            high = high + send(far, "leaf", 2)
            return jnp.concatenate([low, high])

        def root_reduce(make):
            here, arrived = pair_sum(make)
            return plane_reduce(here, arrived, cut_root)

        def root_collect(value):
            blocks = col_collect(value)
            across = jnp.concatenate([send(b, "leaf", 2) for b in blocks])
            near = jnp.concatenate(blocks)
            gathered = [near, across, send(near, "leaf", 1), send(across, "leaf", 1)]
            spots = [
                (((parity ^ i) * 2 + (owner ^ j)) * cols + (col ^ k)) * cut_root
                for i in range(2)
                for j in range(2)
                for k in range(cols)
            ]
            return gathered, ints(spots)

        tile = fit(inverse_leaf.shape[1], 256)
        leaf_part = product(
            inverse_leaf,
            terms=[(rhs_leaf[0], 1)],
            tile_r=tiles(inverse_leaf.shape[1] // tile),
            tile=tile,
        )
        forward_leaf = row_terms(leaf_part)

        def make_mid(i):
            tile = fit(split, 512)
            granule = min(cut_mid, unit)
            return product(
                factor_leaf_mid,
                terms=forward_leaf,
                pattern=pattern_leaf_mid,
                tile_r=tiles(split // tile, half_start(i, tile)),
                tile=tile,
                granule=granule,
                dst=order(cut_mid, granule, False),
            )

        here, arrived = pair_sum(make_mid)
        summed = here + arrived
        to_mid = col_reduce([summed[k * cut_mid : (k + 1) * cut_mid] for k in range(cols)])
        own_rhs = lax.dynamic_slice(
            rhs_mid, (owner, parity * split + col * cut_mid, 0), (1, cut_mid, 128)
        )[0]
        blocks = col_collect(own_rhs - to_mid)
        across = jnp.concatenate([send(b, "leaf", 2) for b in blocks])
        near = jnp.concatenate(blocks)
        mid_pieces = [near, across, send(near, "leaf", 1), send(across, "leaf", 1)]
        mid_offs = ints(
            [
                (owner ^ j) * full + (parity ^ i) * split + (col ^ k) * cut_mid
                for i in range(2)
                for j in range(2)
                for k in range(cols)
            ]
        )

        def make_leaf_root(i):
            tile = fit(split, 512)
            granule = min(cut_root, unit)
            return product(
                factor_leaf_root,
                terms=forward_leaf,
                pattern=pattern_leaf_root,
                tile_r=tiles(split // tile, half_start(i, tile)),
                tile=tile,
                granule=granule,
                dst=order(cut_root, granule, True),
            )

        leaf_root_parts = [make_leaf_root(0), make_leaf_root(1)]

        tile = fit(own, 256)
        mid_part = product(
            inverse_mid,
            pieces=mid_pieces,
            piece=cut_mid,
            offs=mid_offs,
            vectors=2,
            tile_p=ints([p for p in range(2) for _ in range(own // tile)]),
            tile_r=ints([n for _ in range(2) for n in range(own // tile)]),
            tile=tile,
        )
        forward_mid = row_terms(mid_part)

        def make_root(i):
            tile = fit(split, 1024)
            granule = min(cut_root, unit)
            return product(
                factor_mid_root,
                terms=forward_mid,
                pattern=pattern_mid_root,
                vectors=2,
                sum_p=True,
                tile_r=tiles(split // tile, half_start(i, tile)),
                tile=tile,
                granule=granule,
                dst=order(cut_root, granule, True),
                addend=leaf_root_parts[i],
            )

        to_root = root_reduce(make_root)
        offset = ((parity * 2 + owner) * cols + col) * cut_root
        own_rhs = lax.dynamic_slice(rhs_root, (offset, 0), (cut_root, 128))
        root_pieces, root_offs = root_collect(own_rhs - to_root)
        tile = fit(own, 256)
        root_part = product(
            inverse_root,
            pieces=root_pieces,
            piece=cut_root,
            offs=root_offs,
            tile_r=tiles(own // tile),
            tile=tile,
        )
        root_terms = row_terms(root_part)
        forward_root = total(root_terms)

        def make_back_root(i):
            tile = fit(split, 1024)
            granule = min(cut_root, unit)
            return product(
                inverse_root,
                transposed=True,
                terms=root_terms,
                tile_r=tiles(split // tile, half_start(i, tile)),
                tile=tile,
                granule=granule,
                dst=order(cut_root, granule, True),
            )

        root_pieces, root_offs = root_collect(root_reduce(make_back_root))
        tile = fit(own, 256)
        mid_back, solve_root = product(
            factor_mid_root,
            transposed=True,
            pieces=root_pieces,
            piece=cut_root,
            offs=root_offs,
            pattern=pattern_mid_root,
            tile_p=ints([p for p in range(2) for _ in range(own // tile)]),
            tile_r=ints([n for _ in range(2) for n in range(own // tile)]),
            tile=tile,
            ordered=True,
        )
        corrected_mid = forward_mid + row_terms(mid_back, -1)

        def make_back_mid(i):
            tile = fit(split, 1024)
            granule = min(cut_mid, unit)
            count = split // tile
            return product(
                inverse_mid,
                transposed=True,
                terms=corrected_mid,
                vectors=2,
                tile_p=ints([p for p in range(2) for _ in range(count)]),
                tile_r=jnp.tile(tiles(count, half_start(i, tile)), 2),
                tile=tile,
                granule=granule,
                dst=order(cut_mid, granule, True),
            )

        here, arrived = pair_sum(make_back_mid)
        mid_piece = plane_reduce(here, arrived, cut_mid)
        near = jnp.concatenate(col_collect(mid_piece))
        tile = fit(factor_leaf_root.shape[2], 256)
        leaf_tiles = tiles(factor_leaf_root.shape[2] // tile)
        back_part = product(
            factor_leaf_root,
            transposed=True,
            terms=[(solve_root, 1)],
            pattern=pattern_leaf_root,
            tile_r=leaf_tiles,
            tile=tile,
        )
        back_part, mid_own = product(
            factor_leaf_mid,
            transposed=True,
            pieces=[near, send(near, "leaf", 1)],
            piece=cut_mid,
            offs=ints(
                [(parity ^ i) * split + (col ^ k) * cut_mid for i in range(2) for k in range(cols)]
            ),
            pattern=pattern_leaf_mid,
            tile_r=leaf_tiles,
            tile=tile,
            addend=back_part,
            ordered=True,
        )
        corrected_leaf = total(forward_leaf + row_terms(back_part, -1))
        mid_other = send(mid_own, "leaf", 2)
        solve_mid = jnp.where(
            owner == 0, jnp.stack([mid_own, mid_other]), jnp.stack([mid_other, mid_own])
        )
        cut_leaf = full // cols
        tile = fit(cut_leaf, 512)

        def make_leaf(k):
            count = cut_leaf // tile
            return product(
                inverse_leaf,
                transposed=True,
                terms=[(corrected_leaf, 1)],
                tile_r=tiles(count, (col ^ k) * count),
                tile=tile,
            )

        away = [(k, send(make_leaf(k), "col", k)) for k in range(1, cols)]
        leaf_piece = make_leaf(0)
        for _, block in away:
            leaf_piece = leaf_piece + block
        solve_leaf = jnp.zeros((cols, cut_leaf, 128), FULL)
        for k, block in enumerate(col_collect(leaf_piece)):
            solve_leaf = lax.dynamic_update_index_in_dim(solve_leaf, block, col ^ k, 0)
        return (solve_leaf.reshape(1, full, 128), solve_mid, solve_root, forward_root)

    return shards


def solution(mesh):
    return jax.shard_map(
        make_shards(dict(mesh.shape)),
        mesh=mesh,
        in_specs=(
            P("leaf", "row", None),
            P(None, "row", None),
            P("row", None),
            P("leaf", "col", "row"),
            P(None, ("col", "leaf"), "row"),
            P(("col", "leaf"), "row"),
            P("leaf", "row", "col"),
            P("leaf", "row", "col"),
            P(None, "row", ("col", "leaf")),
            P("leaf", "row", "col"),
            P("leaf", "row", "col"),
            P(None, "row", ("col", "leaf")),
        ),
        out_specs=(
            P("leaf", "row", None),
            P(None, "row", None),
            P("row", None),
            P(("col", "leaf"), None),
        ),
        check_vma=False,
    )
```

```python
import functools

import jax
import jax.numpy as jnp
from jax import lax
from jax.experimental import pallas as pl
from jax.experimental.pallas import tpu as pltpu
from jax.sharding import PartitionSpec as P

HALF = jnp.bfloat16
FULL = jnp.float32


def product_kernel(cfg, *refs):
    refs = list(refs)
    tile_p, tile_r, dst, offs, pattern = refs[:5]
    streams = cfg["streams"]
    matrices = refs[5 : 5 + streams]
    at = 5 + streams
    terms = refs[at : at + len(cfg["signs"])]
    at += len(cfg["signs"])
    pieces = refs[at : at + cfg["pieces"]]
    at += cfg["pieces"]
    addend = refs[at] if cfg["addend"] else None
    at += 1 if cfg["addend"] else 0
    out = refs[at]
    at += 1
    ordered = refs[at] if cfg["ordered"] else None
    at += 1 if cfg["ordered"] else 0
    vector = refs[at]
    transposed, depth, vectors = cfg["transposed"], cfg["depth"], cfg["vectors"]
    step = pl.program_id(0)

    @pl.when(step == 0)
    def _():
        if pieces:
            target = ordered if transposed else vector
            count = 0
            for piece in pieces:
                size = cfg["piece"]
                for n in range(piece.shape[0] // size):
                    row = pl.multiple_of(offs[count], size)
                    target[pl.ds(row, size), :] = piece[pl.ds(n * size, size), :].astype(
                        target.dtype
                    )
                    count += 1
        chunk = min(512, depth)
        for base in range(0, vectors * depth, chunk):
            if pieces:
                if not transposed:
                    break
                value = ordered[pl.ds(base, chunk), :]
            else:
                value = None
                for term, sign in zip(terms, cfg["signs"]):
                    part = term[pl.ds(base, chunk), :].astype(FULL)
                    if value is None:
                        value = part
                    else:
                        value = value + part if sign > 0 else value - part
            if transposed:
                slot, column = base // depth, base % depth
                vector[pl.ds(slot * 128, 128), pl.ds(column, chunk)] = value.T.astype(HALF)
            else:
                vector[pl.ds(base, chunk), :] = value.astype(HALF)

    tile, granule, block = cfg["tile"], cfg["granule"], cfg["block"]
    blocks_r, blocks_c, other = cfg["blocks_r"], cfg["blocks_c"], cfg["other"]
    for sub in range(tile // block):
        result = None
        for lead, which in [(p, n) for p in range(matrices[0].shape[0]) for n in range(streams)]:
            matrix = matrices[which]
            share = depth // streams
            index = lead if cfg["sum_p"] else tile_p[step]
            start = 0
            if vectors > 1:
                stride = 128 if transposed else depth
                start = index * stride
                if not cfg["sum_p"]:
                    start = pl.multiple_of(start, stride)
            if transposed:
                x = vector[pl.ds(start, 128), pl.ds(which * share, share)]
                a = matrix[lead, :, pl.ds(sub * block, block)]
            else:
                start = start + which * share
                if vectors > 1 and not cfg["sum_p"]:
                    start = pl.multiple_of(start, share)
                x = vector[pl.ds(start, share), :]
                a = matrix[lead, pl.ds(sub * block, block), :]
            if cfg["masked"]:
                here = (tile_r[step] * tile + sub * block) // cfg["pattern_block"]
                kept = []
                for n in range(share // other):
                    across = which * (share // other) + n
                    if transposed:
                        flag = pattern[(index * blocks_r + across) * blocks_c + here]
                        part = x[:, n * other : (n + 1) * other]
                    else:
                        flag = pattern[(index * blocks_r + here) * blocks_c + across]
                        part = x[n * other : (n + 1) * other, :]
                    kept.append(jnp.where(flag != 0, part, jnp.zeros_like(part)))
                if len(kept) > 1:
                    x = jnp.concatenate(kept, axis=1 if transposed else 0)
                else:
                    x = kept[0]
            if transposed:
                term = jnp.dot(x, a, preferred_element_type=FULL)
            else:
                term = jnp.dot(a, x, preferred_element_type=FULL)
            result = term if result is None else result + term
        if transposed:
            result = result.T
        for g in range(block // granule):
            row = pl.multiple_of(dst[step * (tile // granule) + sub * (block // granule) + g], granule)
            value = result[g * granule : (g + 1) * granule, :]
            if addend is not None:
                value = value + addend[pl.ds(row, granule), :]
            out[pl.ds(row, granule), :] = value


def product(
    matrix,
    *,
    transposed=False,
    terms=(),
    pieces=(),
    piece=0,
    offs=None,
    tile_p=None,
    tile_r=None,
    tile=None,
    dst=None,
    granule=None,
    pattern=None,
    sum_p=False,
    addend=None,
    ordered=False,
    vectors=1,
):
    lead, rows, cols = matrix.shape
    extent, depth = (cols, rows) if transposed else (rows, cols)
    tiles = tile_r.shape[0]
    out_rows = tiles * tile
    masked = pattern is not None
    block, other, pattern_block = tile, depth, tile
    blocks_r = blocks_c = 1
    if masked:
        blocks_r, blocks_c = pattern.shape[1:]
        pattern_block = extent // (blocks_c if transposed else blocks_r)
        other = depth // (blocks_r if transposed else blocks_c)
        block = min(tile, pattern_block)
        flags = pattern.reshape(-1)
    else:
        flags = jnp.zeros((8,), jnp.int32)
        if transposed:
            block = min(tile, 256)
    granule = min(granule or block, block)
    if dst is None:
        dst = jnp.arange(out_rows // granule, dtype=jnp.int32) * granule
    if offs is None:
        offs = jnp.zeros((8,), jnp.int32)
    if tile_p is None:
        tile_p = jnp.zeros((tiles,), jnp.int32)
    least = other if masked else 128
    streams = max([1] + [n for n in (2, 4) if depth % (n * least) == 0])
    signs = tuple(sign for _, sign in terms)
    term_arrays = [array for array, _ in terms]
    x_rows = vectors * depth
    cfg = dict(
        transposed=transposed, depth=depth, vectors=vectors, signs=signs, pieces=len(pieces),
        piece=piece, addend=addend is not None, ordered=ordered, tile=tile, granule=granule,
        block=block, other=other, pattern_block=pattern_block, blocks_r=blocks_r,
        blocks_c=blocks_c, masked=masked, sum_p=sum_p, streams=streams,
    )
    held = lead if sum_p else 1
    share = depth // streams
    if transposed:
        matrix_block = (held, share, tile)
        maps = [lambda t, tp, tr, *_, s=s: (tp[t], s, tr[t]) for s in range(streams)]
    else:
        matrix_block = (held, tile, share)
        maps = [lambda t, tp, tr, *_, s=s: (tp[t], tr[t], s) for s in range(streams)]

    def whole(array):
        return pl.BlockSpec(array.shape, lambda t, *_: (0, 0), pipeline_mode=pl.Buffered(1))

    inputs = term_arrays + list(pieces) + ([addend] if addend is not None else [])
    out_shape = [jax.ShapeDtypeStruct((out_rows, 128), FULL)]
    out_specs = [pl.BlockSpec((out_rows, 128), lambda t, *_: (0, 0))]
    if ordered:
        out_shape.append(jax.ShapeDtypeStruct((x_rows, 128), FULL))
        out_specs.append(pl.BlockSpec((x_rows, 128), lambda t, *_: (0, 0)))
    scratch = (vectors * 128, depth) if transposed else (x_rows, 128)
    matrix_bytes = held * depth * tile * 2
    resident = sum(a.size * a.dtype.itemsize for a in inputs)
    written = sum(s.size * 4 for s in out_shape)
    budget = 2 * matrix_bytes + resident + 2 * written + x_rows * 256 + (12 << 20)
    budget = max(budget, 57 << 20)
    result = pl.pallas_call(
        functools.partial(product_kernel, cfg),
        grid_spec=pltpu.PrefetchScalarGridSpec(
            num_scalar_prefetch=5,
            grid=(tiles,),
            in_specs=[pl.BlockSpec(matrix_block, m) for m in maps] + [whole(a) for a in inputs],
            out_specs=out_specs,
            scratch_shapes=[pltpu.VMEM(scratch, HALF)],
        ),
        out_shape=out_shape,
        compiler_params=pltpu.CompilerParams(vmem_limit_bytes=int(budget)),
        cost_estimate=pl.CostEstimate(
            flops=2 * tiles * tile * depth * held * 128,
            bytes_accessed=tiles * matrix_bytes + resident + written,
            transcendentals=0,
        ),
    )(tile_p, tile_r, dst, offs, flags, *[matrix] * streams, *inputs)
    return tuple(result) if ordered else result[0]


def tie_kernel(*refs):
    pass


def tie(value, *others):
    return pl.pallas_call(
        tie_kernel,
        in_specs=[pl.BlockSpec(memory_space=pl.ANY)] * (1 + len(others)),
        out_specs=pl.BlockSpec(memory_space=pl.ANY),
        out_shape=jax.ShapeDtypeStruct(value.shape, value.dtype),
        input_output_aliases={0: 0},
    )(value, *others)


def ints(values):
    return jnp.stack([jnp.asarray(v, jnp.int32) for v in values]).reshape(-1)


def make_shards(sizes):
    rows, cols, leaves = sizes["row"], sizes["col"], sizes["leaf"]

    def send(value, axis, bit):
        size = sizes[axis]
        return lax.ppermute(value, axis, [(i, i ^ bit) for i in range(size)])

    def row_terms(part, sign=1):
        if rows == 2:
            return [(part, sign), (send(part, "row", 1), sign)]
        return [(lax.psum(part, "row"), sign)]

    def total(terms):
        value = terms[0][0]
        for term, sign in terms[1:]:
            value = value + term if sign > 0 else value - term
        return value

    def col_reduce(blocks):
        value = blocks[0]
        for k, block in [(k, send(blocks[k], "col", k)) for k in range(1, cols)]:
            value = value + block
        return value

    def col_collect(value):
        return [value] + [send(value, "col", k) for k in range(1, cols)]

    def shards(
        rhs_leaf,
        rhs_mid,
        rhs_root,
        inverse_leaf,
        inverse_mid,
        inverse_root,
        factor_leaf_mid,
        factor_leaf_root,
        factor_mid_root,
        pattern_leaf_mid,
        pattern_leaf_root,
        pattern_mid_root,
    ):
        leaf = lax.axis_index("leaf")
        col = lax.axis_index("col")
        owner = leaf // 2
        parity = leaf % 2
        inverse_root = inverse_root[None]
        full = rhs_root.shape[0]
        split = full // 2
        cut_mid = split // cols
        cut_root = cut_mid // 2
        own = inverse_mid.shape[1]
        unit = full // pattern_leaf_mid.shape[1]

        def tiles(count, start=0):
            return jnp.arange(count, dtype=jnp.int32) + start

        def fit(extent, limit):
            return min(extent, limit)

        def half_start(i, tile):
            return (parity ^ i) * (split // tile)

        def order(sub, granule, with_pair):
            pairs = 2 if with_pair else 1
            spots = []
            for j in range(pairs):
                for k in range(cols):
                    spot = (((j ^ owner) if with_pair else 0) * cols + (k ^ col)) * sub
                    spots += [spot + n * granule for n in range(sub // granule)]
            return ints(spots)

        def pair_sum(make):
            there = make(1)
            arrived = send(there, "leaf", 1)
            return make(0), arrived

        def plane_reduce(here, arrived, cut):
            shape = (2, cols, cut, 128)
            here, arrived = here.reshape(shape), arrived.reshape(shape)
            first = min(max(8, (2 * cut // 3 + 4) // 8 * 8), cut - 8)
            rest = cut - first

            def part(j, k, low, high):
                return here[j, k, low:high] + arrived[j, k, low:high]

            across = send(
                (here[1, :, :first] + arrived[1, :, :first]).reshape(cols * first, 128), "leaf", 2
            )
            moved = [
                send(
                    (here[:, k, first:] + arrived[:, k, first:]).reshape(2 * rest, 128), "col", k
                )
                for k in range(1, cols)
            ]
            near = [
                part(0, k, 0, first) + across[k * first : (k + 1) * first] for k in range(cols)
            ]
            low = col_reduce(near)
            far = part(1, 0, first, cut)
            high = part(0, 0, first, cut)
            for block in moved:
                far = far + block[rest:]
                high = high + block[:rest]
            high = high + send(far, "leaf", 2)
            return jnp.concatenate([low, high])

        def root_reduce(make):
            here, arrived = pair_sum(make)
            return plane_reduce(here, arrived, cut_root)

        def root_collect(value):
            blocks = col_collect(value)
            across = jnp.concatenate([send(b, "leaf", 2) for b in blocks])
            near = jnp.concatenate(blocks)
            gathered = [near, across, send(near, "leaf", 1), send(across, "leaf", 1)]
            spots = [
                (((parity ^ i) * 2 + (owner ^ j)) * cols + (col ^ k)) * cut_root
                for i in range(2)
                for j in range(2)
                for k in range(cols)
            ]
            return gathered, ints(spots)

        tile = fit(inverse_leaf.shape[1], 256)
        leaf_part = product(
            inverse_leaf,
            terms=[(rhs_leaf[0], 1)],
            tile_r=tiles(inverse_leaf.shape[1] // tile),
            tile=tile,
        )
        forward_leaf = row_terms(leaf_part)

        def make_mid(i):
            tile = fit(split, 512)
            granule = min(cut_mid, unit)
            return product(
                factor_leaf_mid,
                terms=forward_leaf,
                pattern=pattern_leaf_mid,
                tile_r=tiles(split // tile, half_start(i, tile)),
                tile=tile,
                granule=granule,
                dst=order(cut_mid, granule, False),
            )

        here, arrived = pair_sum(make_mid)
        summed = here + arrived
        to_mid = col_reduce([summed[k * cut_mid : (k + 1) * cut_mid] for k in range(cols)])
        own_rhs = lax.dynamic_slice(
            rhs_mid, (owner, parity * split + col * cut_mid, 0), (1, cut_mid, 128)
        )[0]
        def make_leaf_root(i):
            tile = fit(split, 512)
            granule = min(cut_root, unit)
            return product(
                factor_leaf_root,
                terms=forward_leaf,
                pattern=pattern_leaf_root,
                tile_r=tiles(split // tile, half_start(i, tile)),
                tile=tile,
                granule=granule,
                dst=order(cut_root, granule, True),
            )

        leaf_root_parts = [make_leaf_root(0), make_leaf_root(1)]

        blocks = col_collect(tie(own_rhs - to_mid, *leaf_root_parts))
        across = jnp.concatenate([send(b, "leaf", 2) for b in blocks])
        near = jnp.concatenate(blocks)
        mid_pieces = [near, across, send(near, "leaf", 1), send(across, "leaf", 1)]
        mid_offs = ints(
            [
                (owner ^ j) * full + (parity ^ i) * split + (col ^ k) * cut_mid
                for i in range(2)
                for j in range(2)
                for k in range(cols)
            ]
        )

        tile = fit(own, 256)
        mid_part = product(
            inverse_mid,
            pieces=mid_pieces,
            piece=cut_mid,
            offs=mid_offs,
            vectors=2,
            tile_p=ints([p for p in range(2) for _ in range(own // tile)]),
            tile_r=ints([n for _ in range(2) for n in range(own // tile)]),
            tile=tile,
        )
        forward_mid = row_terms(mid_part)

        def make_root(i):
            tile = fit(split, 512)
            granule = min(cut_root, unit)
            return product(
                factor_mid_root,
                terms=forward_mid,
                pattern=pattern_mid_root,
                vectors=2,
                sum_p=True,
                tile_r=tiles(split // tile, half_start(i, tile)),
                tile=tile,
                granule=granule,
                dst=order(cut_root, granule, True),
                addend=leaf_root_parts[i],
            )

        to_root = root_reduce(make_root)
        offset = ((parity * 2 + owner) * cols + col) * cut_root
        own_rhs = lax.dynamic_slice(rhs_root, (offset, 0), (cut_root, 128))
        root_pieces, root_offs = root_collect(own_rhs - to_root)
        tile = fit(own, 256)
        root_part = product(
            inverse_root,
            pieces=root_pieces,
            piece=cut_root,
            offs=root_offs,
            tile_r=tiles(own // tile),
            tile=tile,
        )
        root_terms = row_terms(root_part)
        forward_root = total(root_terms)

        def make_back_root(i):
            tile = fit(split, 1024)
            granule = min(cut_root, unit)
            return product(
                inverse_root,
                transposed=True,
                terms=root_terms,
                tile_r=tiles(split // tile, half_start(i, tile)),
                tile=tile,
                granule=granule,
                dst=order(cut_root, granule, True),
            )

        root_pieces, root_offs = root_collect(root_reduce(make_back_root))
        tile = fit(own, 256)
        mid_back, solve_root = product(
            factor_mid_root,
            transposed=True,
            pieces=root_pieces,
            piece=cut_root,
            offs=root_offs,
            pattern=pattern_mid_root,
            tile_p=ints([p for p in range(2) for _ in range(own // tile)]),
            tile_r=ints([n for _ in range(2) for n in range(own // tile)]),
            tile=tile,
            ordered=True,
        )
        corrected_mid = forward_mid + row_terms(mid_back, -1)

        def make_back_mid(i):
            tile = fit(split, 1024)
            granule = min(cut_mid, unit)
            count = split // tile
            return product(
                inverse_mid,
                transposed=True,
                terms=corrected_mid,
                vectors=2,
                tile_p=ints([p for p in range(2) for _ in range(count)]),
                tile_r=jnp.tile(tiles(count, half_start(i, tile)), 2),
                tile=tile,
                granule=granule,
                dst=order(cut_mid, granule, True),
            )

        here, arrived = pair_sum(make_back_mid)
        mid_piece = plane_reduce(here, arrived, cut_mid)
        tile = fit(factor_leaf_root.shape[2], 256)
        leaf_tiles = tiles(factor_leaf_root.shape[2] // tile)
        back_part = product(
            factor_leaf_root,
            transposed=True,
            terms=[(solve_root, 1)],
            pattern=pattern_leaf_root,
            tile_r=leaf_tiles,
            tile=tile,
        )
        near = jnp.concatenate(col_collect(tie(mid_piece, back_part)))
        back_part, mid_own = product(
            factor_leaf_mid,
            transposed=True,
            pieces=[near, send(near, "leaf", 1)],
            piece=cut_mid,
            offs=ints(
                [(parity ^ i) * split + (col ^ k) * cut_mid for i in range(2) for k in range(cols)]
            ),
            pattern=pattern_leaf_mid,
            tile_r=leaf_tiles,
            tile=tile,
            addend=back_part,
            ordered=True,
        )
        corrected_leaf = total(forward_leaf + row_terms(back_part, -1))
        mid_other = send(mid_own, "leaf", 2)
        solve_mid = jnp.where(
            owner == 0, jnp.stack([mid_own, mid_other]), jnp.stack([mid_other, mid_own])
        )
        cut_leaf = full // cols
        tile = fit(cut_leaf, 512)

        def make_leaf(k):
            count = cut_leaf // tile
            return product(
                inverse_leaf,
                transposed=True,
                terms=[(corrected_leaf, 1)],
                tile_r=tiles(count, (col ^ k) * count),
                tile=tile,
            )

        away = [(k, send(make_leaf(k), "col", k)) for k in range(1, cols)]
        leaf_piece = make_leaf(0)
        for _, block in away:
            leaf_piece = leaf_piece + block
        solve_leaf = jnp.zeros((cols, cut_leaf, 128), FULL)
        for k, block in enumerate(col_collect(leaf_piece)):
            solve_leaf = lax.dynamic_update_index_in_dim(solve_leaf, block, col ^ k, 0)
        return (solve_leaf.reshape(1, full, 128), solve_mid, solve_root, forward_root)

    return shards


def solution(mesh):
    return jax.shard_map(
        make_shards(dict(mesh.shape)),
        mesh=mesh,
        in_specs=(
            P("leaf", "row", None),
            P(None, "row", None),
            P("row", None),
            P("leaf", "col", "row"),
            P(None, ("col", "leaf"), "row"),
            P(("col", "leaf"), "row"),
            P("leaf", "row", "col"),
            P("leaf", "row", "col"),
            P(None, "row", ("col", "leaf")),
            P("leaf", "row", "col"),
            P("leaf", "row", "col"),
            P(None, "row", ("col", "leaf")),
        ),
        out_specs=(
            P("leaf", "row", None),
            P(None, "row", None),
            P("row", None),
            P(("col", "leaf"), None),
        ),
        check_vma=False,
    )
```

```python
import functools

import jax
import jax.numpy as jnp
from jax import lax
from jax.experimental import pallas as pl
from jax.experimental.pallas import tpu as pltpu
from jax.sharding import PartitionSpec as P

HALF = jnp.bfloat16
FULL = jnp.float32


def product_kernel(cfg, *refs):
    refs = list(refs)
    tile_p, tile_r, dst, offs, pattern = refs[:5]
    matrix = refs[5]
    count = len(cfg["signs"]) + cfg["pieces"] + (1 if cfg["addend"] else 0)
    inputs = refs[6 : 6 + count]
    at = 6 + count
    out = refs[at]
    at += 1
    ordered = refs[at] if cfg["ordered"] else None
    at += 1 if cfg["ordered"] else 0
    vector, buffer, arrived = refs[at : at + 3]
    local = refs[at + 3 : at + 3 + count]
    ready = refs[at + 3 + count] if count else None
    terms = local[: len(cfg["signs"])]
    pieces = local[len(cfg["signs"]) : len(cfg["signs"]) + cfg["pieces"]]
    addend = local[-1] if cfg["addend"] else None
    transposed, depth, vectors = cfg["transposed"], cfg["depth"], cfg["vectors"]
    step = pl.program_id(0)
    tile = cfg["tile"]
    height = buffer.shape[1]

    def fetch(t):
        start = pl.multiple_of(tile_r[t] * tile, tile)
        first = 0 if height > 1 or matrix.shape[0] == 1 else tile_p[t]
        if transposed:
            source = matrix.at[pl.ds(first, height), :, pl.ds(start, tile)]
        else:
            source = matrix.at[pl.ds(first, height), pl.ds(start, tile), :]
        return pltpu.make_async_copy(source, buffer.at[t], arrived.at[t])

    def bring(n):
        return pltpu.make_async_copy(inputs[n], local[n], ready.at[n])

    @pl.when(step == 0)
    def _():
        for n in range(count):
            bring(n).start()
        for t in range(cfg["tiles"]):
            fetch(t).start()
        for n in range(count):
            bring(n).wait()
        if pieces:
            target = ordered if transposed else vector
            position = 0
            for piece in pieces:
                size = cfg["piece"]
                for n in range(piece.shape[0] // size):
                    row = pl.multiple_of(offs[position], size)
                    target[pl.ds(row, size), :] = piece[pl.ds(n * size, size), :].astype(
                        target.dtype
                    )
                    position += 1
        chunk = min(512, depth)
        for base in range(0, vectors * depth, chunk):
            if pieces:
                if not transposed:
                    break
                value = ordered[pl.ds(base, chunk), :]
            else:
                value = None
                for term, sign in zip(terms, cfg["signs"]):
                    part = term[pl.ds(base, chunk), :].astype(FULL)
                    if value is None:
                        value = part
                    else:
                        value = value + part if sign > 0 else value - part
            if transposed:
                slot, column = base // depth, base % depth
                vector[pl.ds(slot * 128, 128), pl.ds(column, chunk)] = value.T.astype(HALF)
            else:
                vector[pl.ds(base, chunk), :] = value.astype(HALF)

    fetch(step).wait()
    granule, block = cfg["granule"], cfg["block"]
    blocks_r, blocks_c, other = cfg["blocks_r"], cfg["blocks_c"], cfg["other"]
    for sub in range(tile // block):
        result = None
        for lead in range(height):
            index = lead if cfg["sum_p"] else tile_p[step]
            start = 0
            if vectors > 1:
                stride = 128 if transposed else depth
                start = index * stride
                if not cfg["sum_p"]:
                    start = pl.multiple_of(start, stride)
            if transposed:
                x = vector[pl.ds(start, 128), :]
                a = buffer[step, lead, :, pl.ds(sub * block, block)]
            else:
                x = vector[pl.ds(start, depth), :]
                a = buffer[step, lead, pl.ds(sub * block, block), :]
            if cfg["masked"]:
                here = (tile_r[step] * tile + sub * block) // cfg["pattern_block"]
                kept = []
                for n in range(depth // other):
                    if transposed:
                        flag = pattern[(index * blocks_r + n) * blocks_c + here]
                        part = x[:, n * other : (n + 1) * other]
                    else:
                        flag = pattern[(index * blocks_r + here) * blocks_c + n]
                        part = x[n * other : (n + 1) * other, :]
                    kept.append(jnp.where(flag != 0, part, jnp.zeros_like(part)))
                if len(kept) > 1:
                    x = jnp.concatenate(kept, axis=1 if transposed else 0)
                else:
                    x = kept[0]
            if transposed:
                term = jnp.dot(x, a, preferred_element_type=FULL)
            else:
                term = jnp.dot(a, x, preferred_element_type=FULL)
            result = term if result is None else result + term
        if transposed:
            result = result.T
        for g in range(block // granule):
            row = pl.multiple_of(dst[step * (tile // granule) + sub * (block // granule) + g], granule)
            value = result[g * granule : (g + 1) * granule, :]
            if addend is not None:
                value = value + addend[pl.ds(row, granule), :]
            out[pl.ds(row, granule), :] = value


def product(
    matrix,
    *,
    transposed=False,
    terms=(),
    pieces=(),
    piece=0,
    offs=None,
    tile_p=None,
    tile_r=None,
    tile=None,
    dst=None,
    granule=None,
    pattern=None,
    sum_p=False,
    addend=None,
    ordered=False,
    vectors=1,
):
    lead, rows, cols = matrix.shape
    extent, depth = (cols, rows) if transposed else (rows, cols)
    tiles = tile_r.shape[0]
    out_rows = tiles * tile
    masked = pattern is not None
    block, other, pattern_block = tile, depth, tile
    blocks_r = blocks_c = 1
    if masked:
        blocks_r, blocks_c = pattern.shape[1:]
        pattern_block = extent // (blocks_c if transposed else blocks_r)
        other = depth // (blocks_r if transposed else blocks_c)
        block = min(tile, pattern_block)
        flags = pattern.reshape(-1)
    else:
        flags = jnp.zeros((8,), jnp.int32)
        if transposed:
            block = min(tile, 256)
    granule = min(granule or block, block)
    if dst is None:
        dst = jnp.arange(out_rows // granule, dtype=jnp.int32) * granule
    if offs is None:
        offs = jnp.zeros((8,), jnp.int32)
    if tile_p is None:
        tile_p = jnp.zeros((tiles,), jnp.int32)
    signs = tuple(sign for _, sign in terms)
    term_arrays = [array for array, _ in terms]
    x_rows = vectors * depth
    cfg = dict(
        transposed=transposed, depth=depth, vectors=vectors, signs=signs, pieces=len(pieces),
        piece=piece, addend=addend is not None, ordered=ordered, tile=tile, granule=granule,
        block=block, other=other, pattern_block=pattern_block, blocks_r=blocks_r,
        blocks_c=blocks_c, masked=masked, sum_p=sum_p, tiles=tiles,
    )
    held = lead if sum_p else 1
    matrix_block = (held, depth, tile) if transposed else (held, tile, depth)
    inputs = term_arrays + list(pieces) + ([addend] if addend is not None else [])
    out_shape = [jax.ShapeDtypeStruct((out_rows, 128), FULL)]
    out_specs = [pl.BlockSpec((out_rows, 128), lambda t, *_: (0, 0))]
    if ordered:
        out_shape.append(jax.ShapeDtypeStruct((x_rows, 128), FULL))
        out_specs.append(pl.BlockSpec((x_rows, 128), lambda t, *_: (0, 0)))
    scratch = (vectors * 128, depth) if transposed else (x_rows, 128)
    matrix_bytes = held * depth * tile * 2
    resident = sum(a.size * a.dtype.itemsize for a in inputs)
    written = sum(s.size * 4 for s in out_shape)
    budget = tiles * matrix_bytes + resident + 2 * written + x_rows * 256 + (12 << 20)
    budget = max(budget, 57 << 20)
    result = pl.pallas_call(
        functools.partial(product_kernel, cfg),
        grid_spec=pltpu.PrefetchScalarGridSpec(
            num_scalar_prefetch=5,
            grid=(tiles,),
            in_specs=[pl.BlockSpec(memory_space=pl.ANY)] * (1 + len(inputs)),
            out_specs=out_specs,
            scratch_shapes=[
                pltpu.VMEM(scratch, HALF),
                pltpu.VMEM((tiles,) + matrix_block, HALF),
                pltpu.SemaphoreType.DMA((tiles,)),
            ]
            + [pltpu.VMEM(a.shape, a.dtype) for a in inputs]
            + ([pltpu.SemaphoreType.DMA((len(inputs),))] if inputs else []),
        ),
        out_shape=out_shape,
        compiler_params=pltpu.CompilerParams(vmem_limit_bytes=int(budget)),
        cost_estimate=pl.CostEstimate(
            flops=2 * tiles * tile * depth * held * 128,
            bytes_accessed=tiles * matrix_bytes + resident + written,
            transcendentals=0,
        ),
    )(tile_p, tile_r, dst, offs, flags, matrix, *inputs)
    return tuple(result) if ordered else result[0]


def tie_kernel(*refs):
    pass


def tie(value, *others):
    return pl.pallas_call(
        tie_kernel,
        in_specs=[pl.BlockSpec(memory_space=pl.ANY)] * (1 + len(others)),
        out_specs=pl.BlockSpec(memory_space=pl.ANY),
        out_shape=jax.ShapeDtypeStruct(value.shape, value.dtype),
        input_output_aliases={0: 0},
    )(value, *others)


def ints(values):
    return jnp.stack([jnp.asarray(v, jnp.int32) for v in values]).reshape(-1)


def make_shards(sizes):
    rows, cols, leaves = sizes["row"], sizes["col"], sizes["leaf"]

    def send(value, axis, bit):
        size = sizes[axis]
        return lax.ppermute(value, axis, [(i, i ^ bit) for i in range(size)])

    def row_terms(part, sign=1):
        if rows == 2:
            return [(part, sign), (send(part, "row", 1), sign)]
        return [(lax.psum(part, "row"), sign)]

    def total(terms):
        value = terms[0][0]
        for term, sign in terms[1:]:
            value = value + term if sign > 0 else value - term
        return value

    def col_reduce(blocks):
        value = blocks[0]
        for k, block in [(k, send(blocks[k], "col", k)) for k in range(1, cols)]:
            value = value + block
        return value

    def col_collect(value):
        return [value] + [send(value, "col", k) for k in range(1, cols)]

    def shards(
        rhs_leaf,
        rhs_mid,
        rhs_root,
        inverse_leaf,
        inverse_mid,
        inverse_root,
        factor_leaf_mid,
        factor_leaf_root,
        factor_mid_root,
        pattern_leaf_mid,
        pattern_leaf_root,
        pattern_mid_root,
    ):
        leaf = lax.axis_index("leaf")
        col = lax.axis_index("col")
        owner = leaf // 2
        parity = leaf % 2
        inverse_root = inverse_root[None]
        full = rhs_root.shape[0]
        split = full // 2
        cut_mid = split // cols
        cut_root = cut_mid // 2
        own = inverse_mid.shape[1]
        unit = full // pattern_leaf_mid.shape[1]

        def tiles(count, start=0):
            return jnp.arange(count, dtype=jnp.int32) + start

        def fit(extent, limit):
            return min(extent, limit)

        def half_start(i, tile):
            return (parity ^ i) * (split // tile)

        def order(sub, granule, with_pair):
            pairs = 2 if with_pair else 1
            spots = []
            for j in range(pairs):
                for k in range(cols):
                    spot = (((j ^ owner) if with_pair else 0) * cols + (k ^ col)) * sub
                    spots += [spot + n * granule for n in range(sub // granule)]
            return ints(spots)

        def pair_sum(make):
            there = make(1)
            arrived = send(there, "leaf", 1)
            return make(0), arrived

        def plane_reduce(here, arrived, cut):
            shape = (2, cols, cut, 128)
            here, arrived = here.reshape(shape), arrived.reshape(shape)
            first = min(max(8, (2 * cut // 3 + 4) // 8 * 8), cut - 8)
            rest = cut - first

            def part(j, k, low, high):
                return here[j, k, low:high] + arrived[j, k, low:high]

            across = send(
                (here[1, :, :first] + arrived[1, :, :first]).reshape(cols * first, 128), "leaf", 2
            )
            moved = [
                send(
                    (here[:, k, first:] + arrived[:, k, first:]).reshape(2 * rest, 128), "col", k
                )
                for k in range(1, cols)
            ]
            near = [
                part(0, k, 0, first) + across[k * first : (k + 1) * first] for k in range(cols)
            ]
            low = col_reduce(near)
            far = part(1, 0, first, cut)
            high = part(0, 0, first, cut)
            for block in moved:
                far = far + block[rest:]
                high = high + block[:rest]
            high = high + send(far, "leaf", 2)
            return jnp.concatenate([low, high])

        def root_reduce(make):
            here, arrived = pair_sum(make)
            return plane_reduce(here, arrived, cut_root)

        def root_collect(value):
            blocks = col_collect(value)
            across = jnp.concatenate([send(b, "leaf", 2) for b in blocks])
            near = jnp.concatenate(blocks)
            gathered = [near, across, send(near, "leaf", 1), send(across, "leaf", 1)]
            spots = [
                (((parity ^ i) * 2 + (owner ^ j)) * cols + (col ^ k)) * cut_root
                for i in range(2)
                for j in range(2)
                for k in range(cols)
            ]
            return gathered, ints(spots)

        tile = fit(inverse_leaf.shape[1], 256)
        leaf_part = product(
            inverse_leaf,
            terms=[(rhs_leaf[0], 1)],
            tile_r=tiles(inverse_leaf.shape[1] // tile),
            tile=tile,
        )
        forward_leaf = row_terms(leaf_part)

        def make_mid(i):
            tile = fit(split, 512)
            granule = min(cut_mid, unit)
            return product(
                factor_leaf_mid,
                terms=forward_leaf,
                pattern=pattern_leaf_mid,
                tile_r=tiles(split // tile, half_start(i, tile)),
                tile=tile,
                granule=granule,
                dst=order(cut_mid, granule, False),
            )

        here, arrived = pair_sum(make_mid)
        summed = here + arrived
        to_mid = col_reduce([summed[k * cut_mid : (k + 1) * cut_mid] for k in range(cols)])
        own_rhs = lax.dynamic_slice(
            rhs_mid, (owner, parity * split + col * cut_mid, 0), (1, cut_mid, 128)
        )[0]
        def make_leaf_root(i):
            tile = fit(split, 512)
            granule = min(cut_root, unit)
            return product(
                factor_leaf_root,
                terms=forward_leaf,
                pattern=pattern_leaf_root,
                tile_r=tiles(split // tile, half_start(i, tile)),
                tile=tile,
                granule=granule,
                dst=order(cut_root, granule, True),
            )

        leaf_root_parts = [make_leaf_root(0), make_leaf_root(1)]

        blocks = col_collect(tie(own_rhs - to_mid, *leaf_root_parts))
        across = jnp.concatenate([send(b, "leaf", 2) for b in blocks])
        near = jnp.concatenate(blocks)
        mid_pieces = [near, across, send(near, "leaf", 1), send(across, "leaf", 1)]
        mid_offs = ints(
            [
                (owner ^ j) * full + (parity ^ i) * split + (col ^ k) * cut_mid
                for i in range(2)
                for j in range(2)
                for k in range(cols)
            ]
        )

        tile = fit(own, 256)
        mid_part = product(
            inverse_mid,
            pieces=mid_pieces,
            piece=cut_mid,
            offs=mid_offs,
            vectors=2,
            tile_p=ints([p for p in range(2) for _ in range(own // tile)]),
            tile_r=ints([n for _ in range(2) for n in range(own // tile)]),
            tile=tile,
        )
        forward_mid = row_terms(mid_part)

        def make_root(i):
            tile = fit(split, 512)
            granule = min(cut_root, unit)
            return product(
                factor_mid_root,
                terms=forward_mid,
                pattern=pattern_mid_root,
                vectors=2,
                sum_p=True,
                tile_r=tiles(split // tile, half_start(i, tile)),
                tile=tile,
                granule=granule,
                dst=order(cut_root, granule, True),
                addend=leaf_root_parts[i],
            )

        to_root = root_reduce(make_root)
        offset = ((parity * 2 + owner) * cols + col) * cut_root
        own_rhs = lax.dynamic_slice(rhs_root, (offset, 0), (cut_root, 128))
        root_pieces, root_offs = root_collect(own_rhs - to_root)
        tile = fit(own, 256)
        root_part = product(
            inverse_root,
            pieces=root_pieces,
            piece=cut_root,
            offs=root_offs,
            tile_r=tiles(own // tile),
            tile=tile,
        )
        root_terms = row_terms(root_part)
        forward_root = total(root_terms)

        def make_back_root(i):
            tile = fit(split, 1024)
            granule = min(cut_root, unit)
            return product(
                inverse_root,
                transposed=True,
                terms=root_terms,
                tile_r=tiles(split // tile, half_start(i, tile)),
                tile=tile,
                granule=granule,
                dst=order(cut_root, granule, True),
            )

        root_pieces, root_offs = root_collect(root_reduce(make_back_root))
        tile = fit(own, 256)
        mid_back, solve_root = product(
            factor_mid_root,
            transposed=True,
            pieces=root_pieces,
            piece=cut_root,
            offs=root_offs,
            pattern=pattern_mid_root,
            tile_p=ints([p for p in range(2) for _ in range(own // tile)]),
            tile_r=ints([n for _ in range(2) for n in range(own // tile)]),
            tile=tile,
            ordered=True,
        )
        corrected_mid = forward_mid + row_terms(mid_back, -1)

        def make_back_mid(i):
            tile = fit(split, 1024)
            granule = min(cut_mid, unit)
            count = split // tile
            return product(
                inverse_mid,
                transposed=True,
                terms=corrected_mid,
                vectors=2,
                tile_p=ints([p for p in range(2) for _ in range(count)]),
                tile_r=jnp.tile(tiles(count, half_start(i, tile)), 2),
                tile=tile,
                granule=granule,
                dst=order(cut_mid, granule, True),
            )

        here, arrived = pair_sum(make_back_mid)
        mid_piece = plane_reduce(here, arrived, cut_mid)
        tile = fit(factor_leaf_root.shape[2], 256)
        leaf_tiles = tiles(factor_leaf_root.shape[2] // tile)
        back_part = product(
            factor_leaf_root,
            transposed=True,
            terms=[(solve_root, 1)],
            pattern=pattern_leaf_root,
            tile_r=leaf_tiles,
            tile=tile,
        )
        near = jnp.concatenate(col_collect(tie(mid_piece, back_part)))
        back_part, mid_own = product(
            factor_leaf_mid,
            transposed=True,
            pieces=[near, send(near, "leaf", 1)],
            piece=cut_mid,
            offs=ints(
                [(parity ^ i) * split + (col ^ k) * cut_mid for i in range(2) for k in range(cols)]
            ),
            pattern=pattern_leaf_mid,
            tile_r=leaf_tiles,
            tile=tile,
            addend=back_part,
            ordered=True,
        )
        corrected_leaf = total(forward_leaf + row_terms(back_part, -1))
        mid_other = send(mid_own, "leaf", 2)
        solve_mid = jnp.where(
            owner == 0, jnp.stack([mid_own, mid_other]), jnp.stack([mid_other, mid_own])
        )
        cut_leaf = full // cols
        tile = fit(cut_leaf, 512)

        def make_leaf(k):
            count = cut_leaf // tile
            return product(
                inverse_leaf,
                transposed=True,
                terms=[(corrected_leaf, 1)],
                tile_r=tiles(count, (col ^ k) * count),
                tile=tile,
            )

        away = [(k, send(make_leaf(k), "col", k)) for k in range(1, cols)]
        leaf_piece = make_leaf(0)
        for _, block in away:
            leaf_piece = leaf_piece + block
        solve_leaf = jnp.zeros((cols, cut_leaf, 128), FULL)
        for k, block in enumerate(col_collect(leaf_piece)):
            solve_leaf = lax.dynamic_update_index_in_dim(solve_leaf, block, col ^ k, 0)
        return (solve_leaf.reshape(1, full, 128), solve_mid, solve_root, forward_root)

    return shards


def solution(mesh):
    return jax.shard_map(
        make_shards(dict(mesh.shape)),
        mesh=mesh,
        in_specs=(
            P("leaf", "row", None),
            P(None, "row", None),
            P("row", None),
            P("leaf", "col", "row"),
            P(None, ("col", "leaf"), "row"),
            P(("col", "leaf"), "row"),
            P("leaf", "row", "col"),
            P("leaf", "row", "col"),
            P(None, "row", ("col", "leaf")),
            P("leaf", "row", "col"),
            P("leaf", "row", "col"),
            P(None, "row", ("col", "leaf")),
        ),
        out_specs=(
            P("leaf", "row", None),
            P(None, "row", None),
            P("row", None),
            P(("col", "leaf"), None),
        ),
        check_vma=False,
    )
```
